32 devices in a mesh: tm: 8 (over z, x), head: 4 (over y, core).
Axes of the slice: x: 2, y: 2, z: 4, core: 2. Of those that a mesh axis runs over, the one named last changes fastest.
Arguments:
- query_in: bfloat16 [6272, 5120], P('tm', 'head'), may hold values from -6 to 6
- key_in: bfloat16 [6272, 5120], P('tm', 'head'), may hold values from -6 to 6
- value_in: bfloat16 [6272, 5120], P('tm', 'head'), may hold values from -6 to 6
- layer_grad: bfloat16 [6272, 5120], P('tm', 'head'), may hold values from -6 to 6
- out_weight: bfloat16 [5120, 5120], P('head'), may hold values from -0.078125 to 0.078125
- group_mask: int32 [8, 8], replicated, may hold values from 0 to 1, as said below
- first_group: int32 [1], replicated, may hold values from 0 to 7
Outputs:
- query_grad: bfloat16 [6272, 5120], P('tm', 'head')
- key_grad: bfloat16 [6272, 5120], P('tm', 'head')
- value_grad: bfloat16 [6272, 5120], P('tm', 'head')
The draws below stay inside these ranges and needn't reach their ends.
Inputs may be any that keep to these rules, and one draw needn't show every extreme that they name: `group_mask`: 1 on the diagonal; each entry just below the diagonal is 1 or 0; every other entry is 0.
All inputs are finite; a program needn't handle non-finite values.
Results may differ from the reference program's by a relative error of at most 0.015.
Values may be sent and summed in bfloat16 or wider, within the bound.
No kernel may reach another device: no remote copies, remote signals or barrier semaphores. Data moves between devices by JAX's collectives and lax.ppermute only.
A program may use at most 256 MiB of HBM per device.

```python
import jax
import jax.numpy as jnp
from jax import lax

HEADS = 40
D_HEAD = 128
GROUP = 784
WIDTH = 5120
NCHUNK = 8
SEQ = 6272


def draw_query_in(key, part):
    key = jax.random.fold_in(key, 11)
    mixed = jnp.clip(1.5 * jax.random.normal(key, (SEQ, HEADS, D_HEAD), jnp.float32), -6.0, 6.0)
    return mixed.reshape(SEQ, HEADS * D_HEAD).astype(jnp.bfloat16)


def draw_key_in(key, part):
    key = jax.random.fold_in(key, 12)
    mixed = jnp.clip(1.5 * jax.random.normal(key, (SEQ, HEADS, D_HEAD), jnp.float32), -6.0, 6.0)
    return mixed.reshape(SEQ, HEADS * D_HEAD).astype(jnp.bfloat16)


def draw_group_mask(key, part):
    key = jax.random.fold_in(key, 13)
    row_ids = jnp.arange(NCHUNK, dtype=jnp.int32)[:, None]
    col_ids = jnp.arange(NCHUNK, dtype=jnp.int32)[None, :]
    kept = jax.random.randint(key, (NCHUNK, NCHUNK), 0, 2) == 1
    below = (row_ids == col_ids + 1) & kept
    return jnp.where(below | (row_ids == col_ids), 1, 0).astype(jnp.int32)


def block_scale(stream_key, shape, split, smallest, high):
    def one(position, blocks):
        heights = jax.random.uniform(jax.random.fold_in(jax.random.fold_in(stream_key, 6), position), (blocks,), jnp.float32, smallest / len(split), high / len(split))
        return jnp.repeat(jnp.exp(heights), shape[position] // blocks).reshape((-1,) + (1,) * (len(shape) - position - 1))

    gain = one(*split[0])
    for cut in split[1:]:
        gain = gain * one(*cut)
    return gain


def gaussian(own_key, extent, width, most, pieces=(), held_as=jnp.bfloat16):
    loudness = block_scale(own_key, extent, pieces, -0.22, 0.18) if pieces else 1.0
    entries = jax.random.normal(own_key, extent, jnp.float32) * width * loudness
    return jnp.minimum(jnp.maximum(entries, -most), most).astype(held_as)


def setup_inputs(seed: int = 0) -> dict:
    seeds = jax.random.split(jax.random.key(seed), 8)
    return {
        "query_in": draw_query_in(jax.random.fold_in(seeds[7], 71), 0),
        "key_in": draw_key_in(jax.random.fold_in(seeds[7], 71), 0),
        "value_in": gaussian(seeds[2], (SEQ, WIDTH), 1.0, 6.0, ((0, 8), (1, 4))),
        "layer_grad": gaussian(seeds[3], (SEQ, WIDTH), 1.0, 6.0, ((0, 8), (1, 4))),
        "out_weight": gaussian(seeds[4], (WIDTH, WIDTH), WIDTH ** -0.5, 0.078125, ((0, 4),)),
        "group_mask": draw_group_mask(jax.random.fold_in(seeds[7], 71), 0),
        "first_group": jax.random.randint(seeds[6], (1,), 0, NCHUNK).astype(jnp.int32),
    }


lowest_start = -1e30


def reference(query_in, key_in, value_in, layer_grad, out_weight, group_mask, first_group):
    scale = D_HEAD ** -0.5
    attn_grad = jnp.dot(layer_grad, out_weight.T, preferred_element_type=jnp.float32).astype(jnp.bfloat16)
    group_ids = jnp.arange(SEQ, dtype=jnp.int32) // GROUP
    group_ok = (group_mask == 1) | (jnp.arange(NCHUNK, dtype=jnp.int32)[None, :] == first_group[0])

    def by_heads(matrix):
        return matrix.reshape(SEQ, HEADS, D_HEAD).transpose(1, 0, 2)

    def one_head(inputs):
        query_h, key_h, value_h, grad_h = inputs

        def per_block(carry, block_idx):
            key_acc, value_acc = carry
            start = (block_idx * GROUP).astype(jnp.int32)
            query_b = lax.dynamic_slice_in_dim(query_h, start, GROUP, 0)
            grad_b = lax.dynamic_slice_in_dim(grad_h, start, GROUP, 0)
            allowed = group_ok[block_idx][group_ids][None, :]
            scores = scale * jnp.dot(query_b, key_h.T, preferred_element_type=jnp.float32)
            masked = jnp.where(allowed, scores, lowest_start)
            peak = jnp.max(masked, axis=1, keepdims=True)
            total = jnp.sum(jnp.where(allowed, jnp.exp(masked - peak), 0.0), axis=1, keepdims=True)
            log_sum = peak + jnp.log(total)
            probs = jnp.where(allowed, jnp.exp(jnp.where(allowed, scores - log_sum, lowest_start)), 0.0)
            dprobs = jnp.dot(grad_b, value_h.T, preferred_element_type=jnp.float32)
            delta = jnp.sum(probs * dprobs, axis=1, keepdims=True)
            probs_low = probs.astype(jnp.bfloat16)
            value_acc = value_acc + jnp.dot(probs_low.T, grad_b, preferred_element_type=jnp.float32)
            dscores = (probs * (dprobs - delta)).astype(jnp.bfloat16)
            query_part = scale * jnp.dot(dscores, key_h, preferred_element_type=jnp.float32)
            key_acc = key_acc + scale * jnp.dot(dscores.T, query_b, preferred_element_type=jnp.float32)
            return (key_acc, value_acc), query_part

        zeros = jnp.zeros((SEQ, D_HEAD), jnp.float32)
        (key_acc, value_acc), query_parts = lax.scan(per_block, (zeros, zeros), jnp.arange(NCHUNK, dtype=jnp.int32))
        return query_parts.reshape(SEQ, D_HEAD), key_acc, value_acc

    query_all, key_all, value_all = lax.map(one_head, (by_heads(query_in), by_heads(key_in), by_heads(value_in), by_heads(attn_grad)))

    def back(stacked):
        return stacked.transpose(1, 0, 2).reshape(SEQ, HEADS * D_HEAD).astype(jnp.bfloat16)

    return back(query_all), back(key_all), back(value_all)
```

```python
import functools
import math

import jax
import jax.numpy as jnp
from jax import lax
from jax.experimental import pallas as pl
from jax.experimental.pallas import tpu as pltpu
from jax.sharding import PartitionSpec as P

D_HEAD = 128
Q_TILE = 256
PAD = 128
NEVER = 1e30


def nt(a, b):
    return lax.dot_general(a, b, (((1,), (1,)), ((), ())), preferred_element_type=jnp.float32)


def nn(a, b):
    return lax.dot_general(a, b, (((1,), (0,)), ((), ())), preferred_element_type=jnp.float32)


def attn_kernel(
    scale, rows, sub, flags_ref, q_ref, g_ref, ko_ref, vo_ref, near_ref, far_ref, prev_ref, *rest
):
    dq_ref, dko_ref, dvo_ref, dfirst_ref, dprev_ref = rest[-12:-7]
    first_ref, kt_ref, s_ref, dp_ref, pds_ref, dk_acc, dv_acc = rest[-7:]
    log2e = scale * math.log2(math.e)
    is_near = pl.program_id(0) == flags_ref[3]

    @pl.when(is_near)
    def _():
        first_ref[...] = near_ref[...]

    @pl.when(jnp.logical_not(is_near))
    def _():
        first_ref[...] = far_ref[...]

    used = [None, flags_ref[0] > 0, flags_ref[1] > 0]
    keys = [ko_ref, first_ref.at[0], prev_ref.at[0, 0]]
    values = [vo_ref, first_ref.at[1], prev_ref.at[0, 1]]
    for p in range(3):
        kt_ref[p] = keys[p][...].T
    dk_acc[...] = jnp.zeros_like(dk_acc)
    dv_acc[...] = jnp.zeros_like(dv_acc)
    cuts = [pl.ds(j * sub, sub) for j in range(rows // sub)]
    halves = [pl.ds(0, rows)]
    if rows % 32 == 0 or rows // 2 % 8 == 0:
        halves = [pl.ds(0, rows // 2), pl.ds(rows // 2, rows // 2)]

    tiles = []
    for start in range(0, rows, Q_TILE):
        left = min(Q_TILE, rows - start)
        width = -(-left // PAD) * PAD
        at = pl.ds(start, left)
        q_t, g_t = q_ref[at, :], g_ref[at, :]
        if width > left:
            pad = jnp.zeros((width - left, D_HEAD), jnp.bfloat16)
            q_t, g_t = jnp.concatenate([q_t, pad], axis=0), jnp.concatenate([g_t, pad], axis=0)
        tiles.append((at, left, width, q_t, g_t))

    def products(t):
        _, _, width, q_t, g_t = tiles[t]
        slot, lanes = t % 2, pl.ds(0, width)
        for p in range(3):
            for part in halves:
                s_ref[slot, p, part, lanes] = nt(keys[p][part, :], q_t)
                yield
        for p in range(3):
            for part in halves:
                dp_ref[slot, p, part, lanes] = nt(values[p][part, :], g_t)
                yield

    def softmax(t):
        _, _, width, _, _ = tiles[t]
        slot, lanes = t % 2, pl.ds(0, width)
        peak = None
        for p in range(3):
            top = None
            for cut in cuts:
                part = jnp.max(s_ref[slot, p, cut, lanes], axis=0, keepdims=True)
                top = part if top is None else jnp.maximum(top, part)
                yield
            if p > 0:
                top = jnp.where(used[p], top, -NEVER)
            peak = top if peak is None else jnp.maximum(peak, top)
        peak = peak * log2e
        total = jnp.zeros((1, width), jnp.float32)
        dots = jnp.zeros((1, width), jnp.float32)
        for p in range(3):
            shift = peak if p == 0 else jnp.where(used[p], peak, NEVER)
            for cut in cuts:
                e = jnp.exp2(s_ref[slot, p, cut, lanes] * log2e - shift)
                s_ref[slot, p, cut, lanes] = e
                total += jnp.sum(e, axis=0, keepdims=True)
                dots += jnp.sum(e * dp_ref[slot, p, cut, lanes], axis=0, keepdims=True)
                yield
        inv = 1.0 / total
        delta = dots * inv
        for p in range(3):
            for cut in cuts:
                prob = s_ref[slot, p, cut, lanes] * inv
                ds = prob * (dp_ref[slot, p, cut, lanes] - delta)
                pds_ref[slot, 0, p, cut, lanes] = prob.astype(jnp.bfloat16)
                pds_ref[slot, 1, p, cut, lanes] = ds.astype(jnp.bfloat16)
                yield

    def gradients(t):
        at, left, width, q_t, g_t = tiles[t]
        slot, lanes = t % 2, pl.ds(0, width)
        dq_t = jnp.zeros((D_HEAD, width), jnp.float32)
        for p in range(3):
            dv_acc[p] += nn(pds_ref[slot, 0, p, :, lanes], g_t)
            yield
            dk_acc[p] += nn(pds_ref[slot, 1, p, :, lanes], q_t)
            yield
            dq_t += nn(kt_ref[p], pds_ref[slot, 1, p, :, lanes])
            yield
        dq_ref[at, :] = (dq_t * scale).T.astype(jnp.bfloat16)[:left]

    count = len(tiles)
    for stage in range(count + 2):
        live = []
        if stage < count:
            live.append([products(stage), 6 * len(halves), 0])
        if 0 < stage <= count:
            live.append([softmax(stage - 1), 9 * len(cuts), 0])
        if stage > 1:
            live.append([gradients(stage - 2), 9, 0])
        while live:
            turn = min(live, key=lambda x: x[2] / x[1])
            turn[2] += 1
            try:
                next(turn[0])
            except StopIteration:
                live.remove(turn)

    dko_ref[...] = (dk_acc[0] * scale).astype(jnp.bfloat16)
    dvo_ref[...] = dv_acc[0].astype(jnp.bfloat16)
    dfirst_ref[0, 0] = (dk_acc[1] * scale).astype(jnp.bfloat16)
    dfirst_ref[0, 1] = dv_acc[1].astype(jnp.bfloat16)
    dprev_ref[0, 0] = (dk_acc[2] * scale).astype(jnp.bfloat16)
    dprev_ref[0, 1] = dv_acc[2].astype(jnp.bfloat16)


def attn_call(flags, q, g, ko, vo, near, far, prev, outs, heads, scale):
    rows, width = q.shape
    count = len(heads)
    stride = heads[1] - heads[0] if count > 1 else 0
    base = heads[0]
    sub = 112 if rows % 112 == 0 else 16
    column = pl.BlockSpec((rows, D_HEAD), lambda h, f: (0, base + stride * h))
    pair = pl.BlockSpec((1, 2, rows, D_HEAD), lambda h, f: (h, 0, 0, 0))
    both = pl.BlockSpec((2, rows, D_HEAD), lambda h, f: (0, 0, 0))
    whole = jax.ShapeDtypeStruct((rows, width), jnp.bfloat16)
    piece = jax.ShapeDtypeStruct((count, 2, rows, D_HEAD), jnp.bfloat16)
    passed = [] if outs is None else list(outs)
    aliases = {8 + i: i for i in range(len(passed))}
    flops = 2 * 5 * 3 * rows * rows * D_HEAD * count
    return pl.pallas_call(
        functools.partial(attn_kernel, scale, rows, sub),
        grid_spec=pltpu.PrefetchScalarGridSpec(
            num_scalar_prefetch=1,
            grid=(count,),
            in_specs=[column, column, column, column, both, both, pair]
            + [pl.BlockSpec(memory_space=pl.ANY)] * len(passed),
            out_specs=[column, column, column, pair, pair],
            scratch_shapes=[
                pltpu.VMEM((2, rows, D_HEAD), jnp.bfloat16),
                pltpu.VMEM((3, D_HEAD, rows), jnp.bfloat16),
                pltpu.VMEM((2, 3, rows, Q_TILE), jnp.float32),
                pltpu.VMEM((2, 3, rows, Q_TILE), jnp.float32),
                pltpu.VMEM((2, 2, 3, rows, Q_TILE), jnp.bfloat16),
                pltpu.VMEM((3, rows, D_HEAD), jnp.float32),
                pltpu.VMEM((3, rows, D_HEAD), jnp.float32),
            ],
        ),
        out_shape=[whole, whole, whole, piece, piece],
        input_output_aliases=aliases,
        compiler_params=pltpu.CompilerParams(
            dimension_semantics=("arbitrary",), vmem_limit_bytes=44 * 1024 * 1024
        ),
        cost_estimate=pl.CostEstimate(
            flops=2 * flops,
            bytes_accessed=15 * rows * D_HEAD * 2 * count,
            transcendentals=3 * rows * rows * count,
        ),
    )(flags, q, g, ko, vo, near, far, prev, *passed)


def join_kernel(flags_ref, dk_ref, dv_ref, back_ref, near_ref, far_ref, dk_out, dv_out):
    owner = flags_ref[2] > 0
    is_near = pl.program_id(0) == flags_ref[3]
    for i, (src, dst) in enumerate(((dk_ref, dk_out), (dv_ref, dv_out))):
        total = jnp.where(is_near, near_ref[i], far_ref[i]).astype(jnp.float32)
        part = src[...].astype(jnp.float32) + back_ref[0, i].astype(jnp.float32)
        dst[...] = (part + jnp.where(owner, total, 0.0)).astype(jnp.bfloat16)


def join_call(flags, dk, dv, back, near, far, heads):
    rows = dk.shape[0]
    count = len(heads)
    stride = heads[1] - heads[0] if count > 1 else 0
    base = heads[0]
    column = pl.BlockSpec((rows, D_HEAD), lambda h, f: (0, base + stride * h))
    pair = pl.BlockSpec((1, 2, rows, D_HEAD), lambda h, f: (h, 0, 0, 0))
    both = pl.BlockSpec((2, rows, D_HEAD), lambda h, f: (0, 0, 0))
    whole = jax.ShapeDtypeStruct(dk.shape, jnp.bfloat16)
    return pl.pallas_call(
        join_kernel,
        grid_spec=pltpu.PrefetchScalarGridSpec(
            num_scalar_prefetch=1,
            grid=(count,),
            in_specs=[column, column, pair, both, both],
            out_specs=[column, column],
        ),
        out_shape=[whole, whole],
        input_output_aliases={1: 0, 2: 1},
        cost_estimate=pl.CostEstimate(
            flops=4 * rows * D_HEAD * count,
            bytes_accessed=8 * rows * D_HEAD * 2 * count,
            transcendentals=0,
        ),
    )(flags, dk, dv, back, near, far)


def pick(index, candidates):
    keys = sorted(candidates)
    out = candidates[keys[0]]
    for k in keys[1:]:
        out = jnp.where(index == k, candidates[k], out)
    return out


def after(value, *others):
    return lax.optimization_barrier((value, *others))[0]


def local(query_in, key_in, value_in, layer_grad, out_weight, group_mask, first_group):
    rows, width = query_in.shape
    heads = width // D_HEAD
    scale = D_HEAD ** (-0.5)
    n = lax.axis_size("tm")
    me = lax.axis_index("tm")
    first = first_group[0]
    owner = first == me
    prev_index = jnp.maximum(me - 1, 0)
    prev_used = (me > 0) & (group_mask[me, prev_index] == 1) & (first != me - 1)
    lines = n // 2
    line, side = me // 2, me % 2
    source = jnp.where(side == first % 2, first, (first + 1) % n) // 2
    hops = jnp.abs(line - source)
    flags = jnp.stack(
        [(~owner).astype(jnp.int32), prev_used.astype(jnp.int32), owner.astype(jnp.int32), side]
    ).astype(jnp.int32)
    count = heads - heads // 2
    chunks = [tuple(range(c, heads, count)) for c in range(count)]
    forward = [(i, (i + 1) % n) for i in range(n)]
    backward = [(b, a) for a, b in forward]
    higher = [(i, i + 2) for i in range(n - 2)]
    lower = [(b, a) for a, b in higher]
    across = [(i, i ^ 1) for i in range(n)]
    blank = jnp.zeros((2, rows, D_HEAD), jnp.bfloat16)

    def unit(h):
        cols = slice(h * D_HEAD, (h + 1) * D_HEAD)
        return jnp.stack([key_in[:, cols], value_in[:, cols]])

    def half_of(chunk, which):
        low, high = chunk[0], chunk[-1]
        return jnp.where(side == which, low, high)

    gathered = lax.all_gather(layer_grad, "head", axis=1, tiled=True)

    prevs, streams, held = [], [], []
    nears, fars, sums = [], [], []
    outs, attn_grad = None, None
    first_parts, backs = [], []
    shares, ends = [], []
    totals, fetched = [], []

    def send_prev(c):
        units = jnp.stack([unit(h) for h in chunks[c]])
        if c > 1:
            units = after(units, prevs[c - 2])
        got = lax.ppermute(units, "tm", forward)
        prevs.append(got)
        streams.append(jnp.where(owner, half_of(units, 0), half_of(got, 0)))

    def spread(s):
        fresh = streams[s] if s < count else blank
        sent = jnp.where(hops == 0, fresh, held[-1]) if held else fresh
        up = lax.ppermute(sent, "tm", higher)
        down = lax.ppermute(sent, "tm", lower)
        held.append(jnp.where(line > source, up, down))

    def exchange(c):
        near = pick(hops, {0: streams[c], **{d: held[c + d - 1] for d in range(1, lines)}})
        if c > 1:
            near = after(near, first_parts[c - 2])
        nears.append(near)
        fars.append(lax.ppermute(near, "tm", across))

    def attend(c):
        nonlocal outs
        arrived = after(prevs[c], backs[c - 2]) if c > 1 else prevs[c]
        done = attn_call(
            flags, query_in, attn_grad, key_in, value_in, nears[c], fars[c], arrived,
            outs, chunks[c], scale,
        )
        outs = done[:3]
        first_parts.append(done[3])
        backs.append(lax.ppermute(done[4], "tm", backward))
        shares.append(lax.ppermute(half_of(done[3], 1), "tm", across))

    def gather_up(s):
        for c in range(len(sums), min(s + 1, count)):
            mine = half_of(first_parts[c], 0).astype(jnp.float32)
            sums.append(mine + shares[c].astype(jnp.float32))
        low = max(0, s - lines + 1)
        total = pick(s - lines + 1 + hops, {c: sums[c] for c in range(low, min(s, count - 1) + 1)})
        if ends:
            up, down = ends[-1]
            total += jnp.where(line > source, down, up).astype(jnp.float32)
        sent = total.astype(jnp.bfloat16)
        if s >= lines:
            sent = after(sent, fetched[s - lines])
        if s >= count:
            sent = after(sent, backs[min(s - 2, count - 1)])
        ends.append((lax.ppermute(sent, "tm", higher), lax.ppermute(sent, "tm", lower)))
        c = s - lines + 2
        if c >= 0:
            up, down = ends[-1]
            whole = sums[c] + up.astype(jnp.float32) + down.astype(jnp.float32)
            totals.append(whole.astype(jnp.bfloat16))
            fetched.append(lax.ppermute(totals[-1], "tm", backward))

    steps = count + lines - 2
    lead = lines + 1
    for k in range(lead + count + steps + 2):
        if k < count:
            send_prev(k)
        if 0 <= k - 1 < steps:
            spread(k - 1)
        if 0 <= k - lines < count:
            exchange(k - lines)
        if k == lead:
            attn_grad = lax.dot_general(
                after(gathered, nears[0]),
                out_weight,
                (((1,), (1,)), ((), ())),
                preferred_element_type=jnp.float32,
            ).astype(jnp.bfloat16)
        if 0 <= k - lead < count:
            attend(k - lead)
        if 0 <= k - lead - 1 < steps:
            gather_up(k - lead - 1)

    dq, dk, dv = outs
    for c, pair in enumerate(chunks):
        dk, dv = join_call(flags, dk, dv, backs[c], totals[c], fetched[c], pair)
    return dq, dk, dv


def solution(mesh):
    placed = (
        P("tm", "head"),
        P("tm", "head"),
        P("tm", "head"),
        P("tm", "head"),
        P("head", None),
        P(),
        P(),
    )
    return jax.shard_map(
        local,
        mesh=mesh,
        in_specs=placed,
        out_specs=(P("tm", "head"), P("tm", "head"), P("tm", "head")),
        check_vma=False,
    )
```

```python
import functools
import math

import jax
import jax.numpy as jnp
from jax import lax
from jax.experimental import pallas as pl
from jax.experimental.pallas import tpu as pltpu
from jax.sharding import PartitionSpec as P

D_HEAD = 128
Q_TILE = 256
PAD = 128
NEVER = 1e30


def nt(a, b):
    return lax.dot_general(a, b, (((1,), (1,)), ((), ())), preferred_element_type=jnp.float32)


def nn(a, b):
    return lax.dot_general(a, b, (((1,), (0,)), ((), ())), preferred_element_type=jnp.float32)


def attn_kernel(
    scale, rows, sub, flags_ref, q_ref, g_ref, ko_ref, vo_ref, near_ref, far_ref, *rest
):
    befores = rest[:4]
    dq_ref, dko_ref, dvo_ref, dfirst_ref, dprev_ref = rest[-13:-8]
    first_ref, prev_ref, kt_ref, s_ref, dp_ref, pds_ref, dk_acc, dv_acc = rest[-8:]
    log2e = scale * math.log2(math.e)
    is_near = pl.program_id(0) == flags_ref[3]

    @pl.when(is_near)
    def _():
        first_ref[...] = near_ref[0]

    @pl.when(jnp.logical_not(is_near))
    def _():
        first_ref[...] = far_ref[0]

    for which, before_ref in enumerate(befores):

        @pl.when((pl.program_id(0) == which // 2) & (flags_ref[3] == which % 2))
        def _():
            prev_ref[...] = before_ref[0]

    used = [None, flags_ref[0] > 0, flags_ref[1] > 0]
    keys = [ko_ref, first_ref.at[0], prev_ref.at[0]]
    values = [vo_ref, first_ref.at[1], prev_ref.at[1]]
    for p in range(3):
        kt_ref[p] = keys[p][...].T
    dk_acc[...] = jnp.zeros_like(dk_acc)
    dv_acc[...] = jnp.zeros_like(dv_acc)
    cuts = [pl.ds(j * sub, sub) for j in range(rows // sub)]
    halves = [pl.ds(0, rows)]
    if rows % 32 == 0 or rows // 2 % 8 == 0:
        halves = [pl.ds(0, rows // 2), pl.ds(rows // 2, rows // 2)]

    tiles = []
    for start in range(0, rows, Q_TILE):
        left = min(Q_TILE, rows - start)
        width = -(-left // PAD) * PAD
        at = pl.ds(start, left)
        q_t, g_t = q_ref[at, :], g_ref[at, :]
        if width > left:
            pad = jnp.zeros((width - left, D_HEAD), jnp.bfloat16)
            q_t, g_t = jnp.concatenate([q_t, pad], axis=0), jnp.concatenate([g_t, pad], axis=0)
        tiles.append((at, left, width, q_t, g_t))

    def products(t):
        _, _, width, q_t, g_t = tiles[t]
        slot, lanes = t % 2, pl.ds(0, width)
        for p in range(3):
            for part in halves:
                s_ref[slot, p, part, lanes] = nt(keys[p][part, :], q_t)
                yield
        for p in range(3):
            for part in halves:
                dp_ref[slot, p, part, lanes] = nt(values[p][part, :], g_t)
                yield

    def softmax(t):
        _, _, width, _, _ = tiles[t]
        slot, lanes = t % 2, pl.ds(0, width)
        peak = None
        for p in range(3):
            top = None
            for cut in cuts:
                part = jnp.max(s_ref[slot, p, cut, lanes], axis=0, keepdims=True)
                top = part if top is None else jnp.maximum(top, part)
                yield
            if p > 0:
                top = jnp.where(used[p], top, -NEVER)
            peak = top if peak is None else jnp.maximum(peak, top)
        peak = peak * log2e
        total = jnp.zeros((1, width), jnp.float32)
        dots = jnp.zeros((1, width), jnp.float32)
        for p in range(3):
            shift = peak if p == 0 else jnp.where(used[p], peak, NEVER)
            for cut in cuts:
                e = jnp.exp2(s_ref[slot, p, cut, lanes] * log2e - shift)
                s_ref[slot, p, cut, lanes] = e
                total += jnp.sum(e, axis=0, keepdims=True)
                dots += jnp.sum(e * dp_ref[slot, p, cut, lanes], axis=0, keepdims=True)
                yield
        inv = 1.0 / total
        delta = dots * inv
        for p in range(3):
            for cut in cuts:
                prob = s_ref[slot, p, cut, lanes] * inv
                ds = prob * (dp_ref[slot, p, cut, lanes] - delta)
                pds_ref[slot, 0, p, cut, lanes] = prob.astype(jnp.bfloat16)
                pds_ref[slot, 1, p, cut, lanes] = ds.astype(jnp.bfloat16)
                yield

    def gradients(t):
        at, left, width, q_t, g_t = tiles[t]
        slot, lanes = t % 2, pl.ds(0, width)
        dq_t = jnp.zeros((D_HEAD, width), jnp.float32)
        for p in range(3):
            dv_acc[p] += nn(pds_ref[slot, 0, p, :, lanes], g_t)
            yield
            dk_acc[p] += nn(pds_ref[slot, 1, p, :, lanes], q_t)
            yield
            dq_t += nn(kt_ref[p], pds_ref[slot, 1, p, :, lanes])
            yield
        dq_ref[at, :] = (dq_t * scale).T.astype(jnp.bfloat16)[:left]

    count = len(tiles)
    for stage in range(count + 2):
        live = []
        if stage < count:
            live.append([products(stage), 6 * len(halves), 0])
        if 0 < stage <= count:
            live.append([softmax(stage - 1), 9 * len(cuts), 0])
        if stage > 1:
            live.append([gradients(stage - 2), 9, 0])
        while live:
            turn = min(live, key=lambda x: x[2] / x[1])
            turn[2] += 1
            try:
                next(turn[0])
            except StopIteration:
                live.remove(turn)

    dko_ref[...] = (dk_acc[0] * scale).astype(jnp.bfloat16)
    dvo_ref[...] = dv_acc[0].astype(jnp.bfloat16)
    dfirst_ref[0, 0] = (dk_acc[1] * scale).astype(jnp.bfloat16)
    dfirst_ref[0, 1] = dv_acc[1].astype(jnp.bfloat16)
    dprev_ref[0, 0] = (dk_acc[2] * scale).astype(jnp.bfloat16)
    dprev_ref[0, 1] = dv_acc[2].astype(jnp.bfloat16)


def piece_spec(given):
    stack, at = given
    return pl.BlockSpec((1, *stack.shape[1:]), lambda h, f: (at, 0, 0, 0))


def attn_call(flags, q, g, ko, vo, near, far, befores, outs, heads, scale):
    rows, width = q.shape
    count = len(heads)
    stride = heads[1] - heads[0] if count > 1 else 0
    base = heads[0]
    sub = 112 if rows % 112 == 0 else 16
    column = pl.BlockSpec((rows, D_HEAD), lambda h, f: (0, base + stride * h))
    pair = pl.BlockSpec((1, 2, rows, D_HEAD), lambda h, f: (h, 0, 0, 0))
    given = [near, far, *befores]
    whole = jax.ShapeDtypeStruct((rows, width), jnp.bfloat16)
    piece = jax.ShapeDtypeStruct((count, 2, rows, D_HEAD), jnp.bfloat16)
    passed = [] if outs is None else list(outs)
    aliases = {11 + i: i for i in range(len(passed))}
    flops = 2 * 5 * 3 * rows * rows * D_HEAD * count
    return pl.pallas_call(
        functools.partial(attn_kernel, scale, rows, sub),
        grid_spec=pltpu.PrefetchScalarGridSpec(
            num_scalar_prefetch=1,
            grid=(count,),
            in_specs=[column] * 4 + [piece_spec(x) for x in given]
            + [pl.BlockSpec(memory_space=pl.ANY)] * len(passed),
            out_specs=[column, column, column, pair, pair],
            scratch_shapes=[
                pltpu.VMEM((2, rows, D_HEAD), jnp.bfloat16),
                pltpu.VMEM((2, rows, D_HEAD), jnp.bfloat16),
                pltpu.VMEM((3, D_HEAD, rows), jnp.bfloat16),
                pltpu.VMEM((2, 3, rows, Q_TILE), jnp.float32),
                pltpu.VMEM((2, 3, rows, Q_TILE), jnp.float32),
                pltpu.VMEM((2, 2, 3, rows, Q_TILE), jnp.bfloat16),
                pltpu.VMEM((3, rows, D_HEAD), jnp.float32),
                pltpu.VMEM((3, rows, D_HEAD), jnp.float32),
            ],
        ),
        out_shape=[whole, whole, whole, piece, piece],
        input_output_aliases=aliases,
        compiler_params=pltpu.CompilerParams(
            dimension_semantics=("arbitrary",), vmem_limit_bytes=44 * 1024 * 1024
        ),
        cost_estimate=pl.CostEstimate(
            flops=2 * flops,
            bytes_accessed=15 * rows * D_HEAD * 2 * count,
            transcendentals=3 * rows * rows * count,
        ),
    )(flags, q, g, ko, vo, *[x[0] for x in given], *passed)


def join_kernel(flags_ref, dk_ref, dv_ref, *rest):
    backs, total_ref, dk_out, dv_out = rest[:3], rest[3], rest[4], rest[5]
    owner, side, head = flags_ref[2] > 0, flags_ref[3], pl.program_id(0)
    for i, (src, dst) in enumerate(((dk_ref, dk_out), (dv_ref, dv_out))):
        back = jnp.where(side == 0, backs[1][0, i], backs[2][0, i])
        back = jnp.where(head == 0, backs[0][0, i], back).astype(jnp.float32)
        total = jnp.where(owner & (head == side), total_ref[0, i].astype(jnp.float32), 0.0)
        dst[...] = (src[...].astype(jnp.float32) + back + total).astype(jnp.bfloat16)


def join_call(flags, dk, dv, backs, total, heads):
    rows = dk.shape[0]
    count = len(heads)
    stride = heads[1] - heads[0] if count > 1 else 0
    base = heads[0]
    column = pl.BlockSpec((rows, D_HEAD), lambda h, f: (0, base + stride * h))
    given = [*backs, total]
    whole = jax.ShapeDtypeStruct(dk.shape, jnp.bfloat16)
    return pl.pallas_call(
        join_kernel,
        grid_spec=pltpu.PrefetchScalarGridSpec(
            num_scalar_prefetch=1,
            grid=(count,),
            in_specs=[column, column] + [piece_spec(x) for x in given],
            out_specs=[column, column],
        ),
        out_shape=[whole, whole],
        input_output_aliases={1: 0, 2: 1},
        cost_estimate=pl.CostEstimate(
            flops=4 * rows * D_HEAD * count,
            bytes_accessed=8 * rows * D_HEAD * 2 * count,
            transcendentals=0,
        ),
    )(flags, dk, dv, *[x[0] for x in given])


def pick(index, candidates):
    keys = sorted(candidates)
    out = candidates[keys[0]]
    for k in keys[1:]:
        out = jnp.where(index == k, candidates[k], out)
    return out


def after(value, *others):
    return lax.optimization_barrier((value, *others))[0]


def local(query_in, key_in, value_in, layer_grad, out_weight, group_mask, first_group):
    rows, width = query_in.shape
    heads = width // D_HEAD
    scale = D_HEAD ** (-0.5)
    n = lax.axis_size("tm")
    me = lax.axis_index("tm")
    first = first_group[0]
    owner = first == me
    prev_index = jnp.maximum(me - 1, 0)
    prev_used = (me > 0) & (group_mask[me, prev_index] == 1) & (first != me - 1)
    lines = n // 2
    line, side = me // 2, me % 2
    low_side = side == 0
    hops = (line - first // 2) % lines
    beside = first == (me ^ 1)
    flags = jnp.stack(
        [(~owner).astype(jnp.int32), prev_used.astype(jnp.int32), owner.astype(jnp.int32), side]
    ).astype(jnp.int32)
    count = heads - heads // 2
    chunks = [tuple(range(c, heads, count)) for c in range(count)]
    routes = {
        "swap": [(i, i ^ 1) for i in range(n)],
        "up": [(i, (i + 2) % n) for i in range(n)],
        "down": [((i + 2) % n, i) for i in range(n)],
    }
    lead = lines + 1
    steps = count + lines - 2
    f32, bf16 = jnp.float32, jnp.bfloat16

    def unit(h):
        cols = slice(h * D_HEAD, (h + 1) * D_HEAD)
        return jnp.stack([key_in[:, cols], value_in[:, cols]])

    gathered = lax.all_gather(layer_grad, "head", axis=1, tiled=True)

    sent, came, place = {}, {}, {}

    def out(kind, name, k):
        return sent[kind, k], place[name, k]

    def into(kind, name, k):
        return came[kind, k], place[name, k]

    def read(piece):
        return piece[0][piece[1]]

    def has(c):
        return 0 <= c < count

    own = [(unit(pair[0]), unit(pair[-1])) for pair in chunks]
    firsts, prevs, sums, totals = {}, {}, {}, {}
    outs, attn_grad, done = None, None, []

    def swap_parts(k):
        parts = {}
        if has(k):
            parts["a"] = own[k][0]
        if has(k) and has(k - 2):
            parts["b"] = jnp.where(low_side, own[k][1], read(into("up", "next", k - 1)))
        elif has(k):
            parts["b"] = own[k][1]
        elif has(k - 2):
            parts["b"] = read(into("up", "next", k - 1))
        c = k - lines
        if has(c):
            choice = {0: read(out("up", "stream", c + 1))}
            choice.update({d: read(into("up", "stream", c + d)) for d in range(1, lines)})
            parts["first"] = pick(hops, choice)
        c, e = k - lead - 1, k - lead - lines - 1
        if has(c):
            parts["share"] = jnp.where(low_side, firsts[c][-1], firsts[c][0])
        if has(e):
            carried = read(into("down", "sum", k - 1)).astype(f32)
            total = sums[e].astype(f32) + carried
            totals[e] = total.astype(bf16)
            extra = jnp.where(beside, total, 0.0)
            relay = (read(into("down", "back", lead + 2 + e)).astype(f32) + extra).astype(bf16)
            parts["back_a"] = jnp.where(low_side, relay, prevs[e][0])
            high_b = (prevs[e][-1].astype(f32) + extra).astype(bf16)
            parts["back_b"] = jnp.where(low_side, prevs[c][-1], high_b) if has(c) else high_b
        elif has(c):
            parts["back_b"] = prevs[c][-1]
        return parts

    def up_parts(k):
        parts = {}
        c = k - 1
        if has(c):
            parts["next"] = jnp.where(low_side, read(into("swap", "a", c)), own[c][1])
            fresh = jnp.where(
                low_side,
                jnp.where(owner, own[c][0], read(into("swap", "a", c))),
                jnp.where(owner, own[c][1], read(into("swap", "b", c))),
            )
            parts["stream"] = fresh
        if 0 < c < steps:
            passed = read(into("up", "stream", k - 1))
            parts["stream"] = jnp.where(hops == 0, fresh, passed) if has(c) else passed
        return parts

    def down_parts(k):
        parts = {}
        s = k - lead - 2
        if has(s):
            mine = jnp.where(low_side, firsts[s][0], firsts[s][-1]).astype(f32)
            share = read(into("swap", "share", k - 1)).astype(f32)
            sums[s] = after((mine + share).astype(bf16))
            parts["back"] = jnp.where(
                low_side, prevs[s][0], read(into("swap", "back_b", k - 1))
            )
        if 0 <= s < steps:
            low = max(0, s - lines + 1)
            at = s - lines + 1 + hops
            total = pick(at, {c: sums[c] for c in range(low, min(s, count - 1) + 1)})
            if s > 0:
                carried = read(into("down", "sum", k - 1)).astype(f32)
                carried = jnp.where(hops == lines - 1, 0.0, carried)
                total = (total.astype(f32) + carried).astype(bf16)
            parts["sum"] = total
        return parts

    for k in range(lead + count + lines + 2):
        stacks = {}
        for kind, parts in (
            ("swap", swap_parts(k)), ("up", up_parts(k)), ("down", down_parts(k))
        ):
            for i, name in enumerate(parts):
                place[name, k] = i
            if parts:
                stacks[kind] = jnp.stack(list(parts.values()))
        kinds = list(stacks)
        if kinds:
            held = lax.optimization_barrier((*[stacks[x] for x in kinds], *done))
            for kind, stack in zip(kinds, held):
                sent[kind, k] = stack
                came[kind, k] = lax.ppermute(stack, "tm", routes[kind])
        done = []
        ready = [sent[x, k] for x in kinds]
        if k == lines - 1:
            attn_grad = lax.dot_general(
                after(gathered, *ready), out_weight, (((1,), (1,)), ((), ())),
                preferred_element_type=f32,
            ).astype(bf16)
            done.append(attn_grad)
        c = k - lead
        if has(c):
            befores = (
                into("up", "next", c + 1), into("swap", "a", c),
                into("swap", "b", c + 2), into("swap", "b", c),
            )
            results = attn_call(
                after(flags, *ready), query_in, attn_grad, key_in, value_in,
                out("swap", "first", c + lines), into("swap", "first", c + lines),
                befores, outs, chunks[c], scale,
            )
            outs, firsts[c], prevs[c] = results[:3], results[3], results[4]
            done.append(results[3])
        c = k - lead - lines - 2
        if has(c):
            returned = (
                into("swap", "back_a", k - 1), into("swap", "back_b", k - 1),
                into("down", "back", lead + 2 + c),
            )
            dq, dk, dv = outs
            dk, dv = join_call(
                after(flags, *ready) if ready else flags, dk, dv, returned,
                (totals[c][None], 0), chunks[c],
            )
            outs = (dq, dk, dv)
            done.append(dk)
    return tuple(outs)


def solution(mesh):
    placed = (
        P("tm", "head"),
        P("tm", "head"),
        P("tm", "head"),
        P("tm", "head"),
        P("head", None),
        P(),
        P(),
    )
    return jax.shard_map(
        local,
        mesh=mesh,
        in_specs=placed,
        out_specs=(P("tm", "head"), P("tm", "head"), P("tm", "head")),
        check_vma=False,
    )
```

```python
import functools
import math

import jax
import jax.numpy as jnp
from jax import lax
from jax.experimental import pallas as pl
from jax.experimental.pallas import tpu as pltpu
from jax.sharding import PartitionSpec as P

D_HEAD = 128
Q_TILE = 256
PAD = 128
NEVER = 1e30


def nt(a, b):
    return lax.dot_general(a, b, (((1,), (1,)), ((), ())), preferred_element_type=jnp.float32)


def nn(a, b):
    return lax.dot_general(a, b, (((1,), (0,)), ((), ())), preferred_element_type=jnp.float32)


def attn_kernel(
    scale, rows, sub, flags_ref, q_ref, g_ref, ko_ref, vo_ref, near_ref, far_ref, *rest
):
    befores = rest[:4]
    dq_ref, dko_ref, dvo_ref, dfirst_ref, dprev_ref = rest[-13:-8]
    first_ref, prev_ref, kt_ref, s_ref, dp_ref, pds_ref, dk_acc, dv_acc = rest[-8:]
    log2e = scale * math.log2(math.e)
    is_near = pl.program_id(0) == flags_ref[3]

    @pl.when(is_near)
    def _():
        first_ref[...] = near_ref[0]

    @pl.when(jnp.logical_not(is_near))
    def _():
        first_ref[...] = far_ref[0]

    for which, before_ref in enumerate(befores):

        @pl.when((pl.program_id(0) == which // 2) & (flags_ref[3] == which % 2))
        def _():
            prev_ref[...] = before_ref[0]

    used = [None, flags_ref[0] > 0, flags_ref[1] > 0]
    keys = [ko_ref, first_ref.at[0], prev_ref.at[0]]
    values = [vo_ref, first_ref.at[1], prev_ref.at[1]]
    for p in range(3):
        kt_ref[p] = keys[p][...].T
    dk_acc[...] = jnp.zeros_like(dk_acc)
    dv_acc[...] = jnp.zeros_like(dv_acc)
    cuts = [pl.ds(j * sub, sub) for j in range(rows // sub)]
    halves = [pl.ds(0, rows)]
    if rows % 32 == 0 or rows // 2 % 8 == 0:
        halves = [pl.ds(0, rows // 2), pl.ds(rows // 2, rows // 2)]

    tiles = []
    for start in range(0, rows, Q_TILE):
        left = min(Q_TILE, rows - start)
        width = -(-left // PAD) * PAD
        at = pl.ds(start, left)
        q_t, g_t = q_ref[at, :], g_ref[at, :]
        if width > left:
            pad = jnp.zeros((width - left, D_HEAD), jnp.bfloat16)
            q_t, g_t = jnp.concatenate([q_t, pad], axis=0), jnp.concatenate([g_t, pad], axis=0)
        tiles.append((at, left, width, q_t, g_t))

    def products(t):
        _, _, width, q_t, g_t = tiles[t]
        slot, lanes = t % 2, pl.ds(0, width)
        for p in range(3):
            for part in halves:
                s_ref[slot, p, part, lanes] = nt(keys[p][part, :], q_t)
                yield
        for p in range(3):
            for part in halves:
                dp_ref[slot, p, part, lanes] = nt(values[p][part, :], g_t)
                yield

    def softmax(t):
        _, _, width, _, _ = tiles[t]
        slot, lanes = t % 2, pl.ds(0, width)
        peak = None
        for p in range(3):
            top = None
            for cut in cuts:
                part = jnp.max(s_ref[slot, p, cut, lanes], axis=0, keepdims=True)
                top = part if top is None else jnp.maximum(top, part)
                yield
            if p > 0:
                top = jnp.where(used[p], top, -NEVER)
            peak = top if peak is None else jnp.maximum(peak, top)
        peak = peak * log2e
        total = jnp.zeros((1, width), jnp.float32)
        dots = jnp.zeros((1, width), jnp.float32)
        for p in range(3):
            shift = peak if p == 0 else jnp.where(used[p], peak, NEVER)
            for cut in cuts:
                e = jnp.exp2(s_ref[slot, p, cut, lanes] * log2e - shift)
                s_ref[slot, p, cut, lanes] = e
                total += jnp.sum(e, axis=0, keepdims=True)
                dots += jnp.sum(e * dp_ref[slot, p, cut, lanes], axis=0, keepdims=True)
                yield
        inv = 1.0 / total
        delta = dots * inv
        for p in range(3):
            for cut in cuts:
                prob = s_ref[slot, p, cut, lanes] * inv
                ds = prob * (dp_ref[slot, p, cut, lanes] - delta)
                pds_ref[slot, 0, p, cut, lanes] = prob.astype(jnp.bfloat16)
                pds_ref[slot, 1, p, cut, lanes] = ds.astype(jnp.bfloat16)
                yield

    def gradients(t):
        at, left, width, q_t, g_t = tiles[t]
        slot, lanes = t % 2, pl.ds(0, width)
        dq_t = jnp.zeros((D_HEAD, width), jnp.float32)
        for p in range(3):
            dv_acc[p] += nn(pds_ref[slot, 0, p, :, lanes], g_t)
            yield
            dk_acc[p] += nn(pds_ref[slot, 1, p, :, lanes], q_t)
            yield
            dq_t += nn(kt_ref[p], pds_ref[slot, 1, p, :, lanes])
            yield
        dq_ref[at, :] = (dq_t * scale).T.astype(jnp.bfloat16)[:left]

    count = len(tiles)
    for stage in range(count + 2):
        live = []
        if stage < count:
            live.append([products(stage), 6 * len(halves), 0])
        if 0 < stage <= count:
            live.append([softmax(stage - 1), 9 * len(cuts), 0])
        if stage > 1:
            live.append([gradients(stage - 2), 9, 0])
        while live:
            turn = min(live, key=lambda x: x[2] / x[1])
            turn[2] += 1
            try:
                next(turn[0])
            except StopIteration:
                live.remove(turn)

    dko_ref[...] = (dk_acc[0] * scale).astype(jnp.bfloat16)
    dvo_ref[...] = dv_acc[0].astype(jnp.bfloat16)
    dfirst_ref[0, 0] = (dk_acc[1] * scale).astype(jnp.bfloat16)
    dfirst_ref[0, 1] = dv_acc[1].astype(jnp.bfloat16)
    dprev_ref[0, 0] = (dk_acc[2] * scale).astype(jnp.bfloat16)
    dprev_ref[0, 1] = dv_acc[2].astype(jnp.bfloat16)


def piece_spec(given):
    stack, at = given
    return pl.BlockSpec((1, *stack.shape[1:]), lambda h, f: (at, 0, 0, 0))


def attn_call(flags, q, g, ko, vo, near, far, befores, outs, heads, scale):
    rows, width = q.shape
    count = len(heads)
    stride = heads[1] - heads[0] if count > 1 else 0
    base = heads[0]
    sub = 112 if rows % 112 == 0 else 16
    column = pl.BlockSpec((rows, D_HEAD), lambda h, f: (0, base + stride * h))
    pair = pl.BlockSpec((1, 2, rows, D_HEAD), lambda h, f: (h, 0, 0, 0))
    given = [near, far, *befores]
    whole = jax.ShapeDtypeStruct((rows, width), jnp.bfloat16)
    piece = jax.ShapeDtypeStruct((count, 2, rows, D_HEAD), jnp.bfloat16)
    passed = [] if outs is None else list(outs)
    aliases = {11 + i: i for i in range(len(passed))}
    flops = 2 * 5 * 3 * rows * rows * D_HEAD * count
    return pl.pallas_call(
        functools.partial(attn_kernel, scale, rows, sub),
        grid_spec=pltpu.PrefetchScalarGridSpec(
            num_scalar_prefetch=1,
            grid=(count,),
            in_specs=[column] * 4 + [piece_spec(x) for x in given]
            + [pl.BlockSpec(memory_space=pl.ANY)] * len(passed),
            out_specs=[column, column, column, pair, pair],
            scratch_shapes=[
                pltpu.VMEM((2, rows, D_HEAD), jnp.bfloat16),
                pltpu.VMEM((2, rows, D_HEAD), jnp.bfloat16),
                pltpu.VMEM((3, D_HEAD, rows), jnp.bfloat16),
                pltpu.VMEM((2, 3, rows, Q_TILE), jnp.float32),
                pltpu.VMEM((2, 3, rows, Q_TILE), jnp.float32),
                pltpu.VMEM((2, 2, 3, rows, Q_TILE), jnp.bfloat16),
                pltpu.VMEM((3, rows, D_HEAD), jnp.float32),
                pltpu.VMEM((3, rows, D_HEAD), jnp.float32),
            ],
        ),
        out_shape=[whole, whole, whole, piece, piece],
        input_output_aliases=aliases,
        compiler_params=pltpu.CompilerParams(
            dimension_semantics=("arbitrary",), vmem_limit_bytes=58 * 1024 * 1024
        ),
        cost_estimate=pl.CostEstimate(
            flops=2 * flops,
            bytes_accessed=15 * rows * D_HEAD * 2 * count,
            transcendentals=3 * rows * rows * count,
        ),
    )(flags, q, g, ko, vo, *[x[0] for x in given], *passed)


def join_kernel(flags_ref, dk_ref, dv_ref, *rest):
    backs, total_ref, dk_out, dv_out = rest[:3], rest[3], rest[4], rest[5]
    owner, side, head = flags_ref[2] > 0, flags_ref[3], pl.program_id(0)
    for i, (src, dst) in enumerate(((dk_ref, dk_out), (dv_ref, dv_out))):
        back = jnp.where(side == 0, backs[1][0, i], backs[2][0, i])
        back = jnp.where(head == 0, backs[0][0, i], back).astype(jnp.float32)
        total = jnp.where(owner & (head == side), total_ref[0, i].astype(jnp.float32), 0.0)
        dst[...] = (src[...].astype(jnp.float32) + back + total).astype(jnp.bfloat16)


def join_call(flags, dk, dv, backs, total, heads):
    rows = dk.shape[0]
    count = len(heads)
    stride = heads[1] - heads[0] if count > 1 else 0
    base = heads[0]
    column = pl.BlockSpec((rows, D_HEAD), lambda h, f: (0, base + stride * h))
    given = [*backs, total]
    whole = jax.ShapeDtypeStruct(dk.shape, jnp.bfloat16)
    return pl.pallas_call(
        join_kernel,
        grid_spec=pltpu.PrefetchScalarGridSpec(
            num_scalar_prefetch=1,
            grid=(count,),
            in_specs=[column, column] + [piece_spec(x) for x in given],
            out_specs=[column, column],
        ),
        out_shape=[whole, whole],
        input_output_aliases={1: 0, 2: 1},
        cost_estimate=pl.CostEstimate(
            flops=4 * rows * D_HEAD * count,
            bytes_accessed=8 * rows * D_HEAD * 2 * count,
            transcendentals=0,
        ),
    )(flags, dk, dv, *[x[0] for x in given])


def pick(index, candidates):
    keys = sorted(candidates)
    out = candidates[keys[0]]
    for k in keys[1:]:
        out = jnp.where(index == k, candidates[k], out)
    return out


def after(value, *others):
    return lax.optimization_barrier((value, *others))[0]


def local(query_in, key_in, value_in, layer_grad, out_weight, group_mask, first_group):
    rows, width = query_in.shape
    heads = width // D_HEAD
    scale = D_HEAD ** (-0.5)
    n = lax.axis_size("tm")
    me = lax.axis_index("tm")
    first = first_group[0]
    owner = first == me
    prev_index = jnp.maximum(me - 1, 0)
    prev_used = (me > 0) & (group_mask[me, prev_index] == 1) & (first != me - 1)
    lines = n // 2
    line, side = me // 2, me % 2
    low_side = side == 0
    hops = (line - first // 2) % lines
    beside = first == (me ^ 1)
    flags = jnp.stack(
        [(~owner).astype(jnp.int32), prev_used.astype(jnp.int32), owner.astype(jnp.int32), side]
    ).astype(jnp.int32)
    count = heads - heads // 2
    chunks = [tuple(range(c, heads, count)) for c in range(count)]
    routes = {
        "swap": [(i, i ^ 1) for i in range(n)],
        "up": [(i, (i + 2) % n) for i in range(n)],
        "down": [((i + 2) % n, i) for i in range(n)],
    }
    lead = lines + 1
    steps = count + lines - 2
    f32, bf16 = jnp.float32, jnp.bfloat16

    def unit(h):
        cols = slice(h * D_HEAD, (h + 1) * D_HEAD)
        return jnp.stack([key_in[:, cols], value_in[:, cols]])

    gathered = lax.all_gather(layer_grad, "head", axis=1, tiled=True)

    sent, came, place = {}, {}, {}

    def out(kind, name, k):
        return sent[kind, k], place[name, k]

    def into(kind, name, k):
        return came[kind, k], place[name, k]

    def read(piece):
        return piece[0][piece[1]]

    def has(c):
        return 0 <= c < count

    own = [(unit(pair[0]), unit(pair[-1])) for pair in chunks]
    firsts, prevs, sums, totals = {}, {}, {}, {}
    outs, attn_grad, done = None, None, []

    def swap_parts(k):
        parts = {}
        c, e = k - lead - 1, k - lead - lines - 1
        extra = 0.0
        if has(e):
            total = sums[e].astype(f32) + read(into("down", "sum", k - 1)).astype(f32)
            totals[e] = total.astype(bf16)
            extra = jnp.where(beside, total, 0.0)
        low_b = own[k][1] if has(k) else prevs[c][-1] if has(c) else None
        high_b = None
        if has(k - lines):
            high_b = read(into("up", "next", k - 1))
        elif has(e):
            high_b = (prevs[e][-1].astype(f32) + extra).astype(bf16)
        if has(k):
            parts["a"] = own[k][0]
        if low_b is not None and high_b is not None:
            parts["b"] = jnp.where(low_side, low_b, high_b)
        elif low_b is not None or high_b is not None:
            parts["b"] = high_b if low_b is None else low_b
        if has(e):
            relay = (read(into("down", "back", lead + 2 + e)).astype(f32) + extra).astype(bf16)
            parts["back_a"] = jnp.where(low_side, relay, prevs[e][0])
        c = k - lines
        if has(c):
            choice = {0: read(out("up", "stream", c + 1))}
            choice.update({d: read(into("up", "stream", c + d)) for d in range(1, lines)})
            parts["first"] = pick(hops, choice)
        c = k - lead - 1
        if has(c):
            parts["share"] = jnp.where(low_side, firsts[c][-1], firsts[c][0])
        return parts

    def up_parts(k):
        parts = {}
        c = k - 1
        if has(c):
            fresh = jnp.where(
                low_side,
                jnp.where(owner, own[c][0], read(into("swap", "a", c))),
                jnp.where(owner, own[c][1], read(into("swap", "b", c))),
            )
            parts["stream"] = fresh
        if 0 < c < steps:
            passed = read(into("up", "stream", k - 1))
            parts["stream"] = jnp.where(hops == 0, fresh, passed) if has(c) else passed
        c = k - lines + 1
        if has(c):
            parts["next"] = jnp.where(low_side, read(into("swap", "a", c)), own[c][1])
        return parts

    def down_parts(k):
        parts = {}
        s = k - lead - 2
        if has(s):
            mine = jnp.where(low_side, firsts[s][0], firsts[s][-1]).astype(f32)
            share = read(into("swap", "share", k - 1)).astype(f32)
            sums[s] = after((mine + share).astype(bf16))
            parts["back"] = jnp.where(
                low_side, prevs[s][0], read(into("swap", "b", k - 1))
            )
        if 0 <= s < steps:
            low = max(0, s - lines + 1)
            at = s - lines + 1 + hops
            total = pick(at, {c: sums[c] for c in range(low, min(s, count - 1) + 1)})
            if s > 0:
                carried = read(into("down", "sum", k - 1)).astype(f32)
                carried = jnp.where(hops == lines - 1, 0.0, carried)
                total = (total.astype(f32) + carried).astype(bf16)
            parts["sum"] = total
        return parts

    for k in range(lead + count + lines + 2):
        stacks = {}
        for kind, parts in (
            ("swap", swap_parts(k)), ("up", up_parts(k)), ("down", down_parts(k))
        ):
            for i, name in enumerate(parts):
                place[name, k] = i
            if parts:
                stacks[kind] = jnp.stack(list(parts.values()))
        kinds = list(stacks)
        if k >= lines and kinds:
            held = lax.optimization_barrier((*[stacks[x] for x in kinds], *done))
            stacks = dict(zip(kinds, held))
        for kind, stack in stacks.items():
            sent[kind, k] = stack
            came[kind, k] = lax.ppermute(stack, "tm", routes[kind])
        done = []
        ready = [sent[x, k] for x in kinds]
        if k == lines:
            attn_grad = lax.dot_general(
                after(gathered, *ready), out_weight, (((1,), (1,)), ((), ())),
                preferred_element_type=f32,
            ).astype(bf16)
            for kind in kinds:
                came[kind, k] = after(came[kind, k], attn_grad)
        c = k - lead
        if has(c):
            befores = (
                into("up", "next", c + lines - 1), into("swap", "a", c),
                into("swap", "b", c + lines), into("swap", "b", c),
            )
            results = attn_call(
                after(flags, *ready), query_in, attn_grad, key_in, value_in,
                out("swap", "first", c + lines), into("swap", "first", c + lines),
                befores, outs, chunks[c], scale,
            )
            outs, firsts[c], prevs[c] = results[:3], results[3], results[4]
            done.append(results[3])
        c = k - lead - lines - 2
        if has(c):
            returned = (
                into("swap", "back_a", k - 1), into("swap", "b", k - 1),
                into("down", "back", lead + 2 + c),
            )
            dq, dk, dv = outs
            dk, dv = join_call(
                after(flags, *ready) if ready else flags, dk, dv, returned,
                (totals[c][None], 0), chunks[c],
            )
            outs = (dq, dk, dv)
            done.append(dk)
    return tuple(outs)


def solution(mesh):
    placed = (
        P("tm", "head"),
        P("tm", "head"),
        P("tm", "head"),
        P("tm", "head"),
        P("head", None),
        P(),
        P(),
    )
    return jax.shard_map(
        local,
        mesh=mesh,
        in_specs=placed,
        out_specs=(P("tm", "head"), P("tm", "head"), P("tm", "head")),
        check_vma=False,
    )
```

```python
import functools
import math

import jax
import jax.numpy as jnp
from jax import lax
from jax.experimental import pallas as pl
from jax.experimental.pallas import tpu as pltpu
from jax.sharding import PartitionSpec as P

D_HEAD = 128
Q_TILE = 256
PAD = 128
NEVER = 1e30


def nt(a, b):
    return lax.dot_general(a, b, (((1,), (1,)), ((), ())), preferred_element_type=jnp.float32)


def nn(a, b):
    return lax.dot_general(a, b, (((1,), (0,)), ((), ())), preferred_element_type=jnp.float32)


def attn_kernel(
    scale, rows, sub, flags_ref, q_ref, g_ref, ko_ref, vo_ref, near_ref, far_ref, *rest
):
    befores = rest[:4]
    dq_ref, dko_ref, dvo_ref, dfirst_ref, dprev_ref = rest[-13:-8]
    first_ref, prev_ref, kt_ref, s_ref, dp_ref, pds_ref, dk_acc, dv_acc = rest[-8:]
    log2e = scale * math.log2(math.e)
    is_near = pl.program_id(0) == flags_ref[3]

    @pl.when(is_near)
    def _():
        first_ref[...] = near_ref[0]

    @pl.when(jnp.logical_not(is_near))
    def _():
        first_ref[...] = far_ref[0]

    for which, before_ref in enumerate(befores):

        @pl.when((pl.program_id(0) == which // 2) & (flags_ref[3] == which % 2))
        def _():
            prev_ref[...] = before_ref[0]

    used = [None, flags_ref[0] > 0, flags_ref[1] > 0]
    keys = [ko_ref, first_ref.at[0], prev_ref.at[0]]
    values = [vo_ref, first_ref.at[1], prev_ref.at[1]]
    for p in range(3):
        kt_ref[p] = keys[p][...].T
    dk_acc[...] = jnp.zeros_like(dk_acc)
    dv_acc[...] = jnp.zeros_like(dv_acc)
    cuts = [pl.ds(j * sub, sub) for j in range(rows // sub)]
    halves = [pl.ds(0, rows)]
    if rows % 32 == 0 or rows // 2 % 8 == 0:
        halves = [pl.ds(0, rows // 2), pl.ds(rows // 2, rows // 2)]

    tiles = []
    for start in range(0, rows, Q_TILE):
        left = min(Q_TILE, rows - start)
        width = -(-left // PAD) * PAD
        at = pl.ds(start, left)
        q_t, g_t = q_ref[at, :], g_ref[at, :]
        if width > left:
            pad = jnp.zeros((width - left, D_HEAD), jnp.bfloat16)
            q_t, g_t = jnp.concatenate([q_t, pad], axis=0), jnp.concatenate([g_t, pad], axis=0)
        tiles.append((at, left, width, q_t, g_t))

    def products(t):
        _, _, width, q_t, g_t = tiles[t]
        slot, lanes = t % 2, pl.ds(0, width)
        for p in range(3):
            for part in halves:
                s_ref[slot, p, part, lanes] = nt(keys[p][part, :], q_t)
                yield
        for p in range(3):
            for part in halves:
                dp_ref[slot, p, part, lanes] = nt(values[p][part, :], g_t)
                yield

    def softmax(t):
        _, _, width, _, _ = tiles[t]
        slot, lanes = t % 2, pl.ds(0, width)
        peak = None
        for p in range(3):
            top = None
            for cut in cuts:
                part = jnp.max(s_ref[slot, p, cut, lanes], axis=0, keepdims=True)
                top = part if top is None else jnp.maximum(top, part)
                yield
            if p > 0:
                top = jnp.where(used[p], top, -NEVER)
            peak = top if peak is None else jnp.maximum(peak, top)
        peak = peak * log2e
        total = jnp.zeros((1, width), jnp.float32)
        dots = jnp.zeros((1, width), jnp.float32)
        for p in range(3):
            shift = peak if p == 0 else jnp.where(used[p], peak, NEVER)
            for cut in cuts:
                e = jnp.exp2(s_ref[slot, p, cut, lanes] * log2e - shift)
                s_ref[slot, p, cut, lanes] = e
                total += jnp.sum(e, axis=0, keepdims=True)
                dots += jnp.sum(e * dp_ref[slot, p, cut, lanes], axis=0, keepdims=True)
                yield
        inv = 1.0 / total
        delta = dots * inv
        for p in range(3):
            for cut in cuts:
                prob = s_ref[slot, p, cut, lanes] * inv
                ds = prob * (dp_ref[slot, p, cut, lanes] - delta)
                pds_ref[slot, 0, p, cut, lanes] = prob.astype(jnp.bfloat16)
                pds_ref[slot, 1, p, cut, lanes] = ds.astype(jnp.bfloat16)
                yield

    def gradients(t):
        at, left, width, q_t, g_t = tiles[t]
        slot, lanes = t % 2, pl.ds(0, width)
        dq_t = jnp.zeros((D_HEAD, width), jnp.float32)
        for p in range(3):
            dv_acc[p] += nn(pds_ref[slot, 0, p, :, lanes], g_t)
            yield
            dk_acc[p] += nn(pds_ref[slot, 1, p, :, lanes], q_t)
            yield
            dq_t += nn(kt_ref[p], pds_ref[slot, 1, p, :, lanes])
            yield
        dq_ref[at, :] = (dq_t * scale).T.astype(jnp.bfloat16)[:left]

    count = len(tiles)
    for stage in range(count + 2):
        live = []
        if stage < count:
            live.append([products(stage), 6 * len(halves), 0])
        if 0 < stage <= count:
            live.append([softmax(stage - 1), 9 * len(cuts), 0])
        if stage > 1:
            live.append([gradients(stage - 2), 9, 0])
        while live:
            turn = min(live, key=lambda x: x[2] / x[1])
            turn[2] += 1
            try:
                next(turn[0])
            except StopIteration:
                live.remove(turn)

    dko_ref[...] = (dk_acc[0] * scale).astype(jnp.bfloat16)
    dvo_ref[...] = dv_acc[0].astype(jnp.bfloat16)
    dfirst_ref[0, 0] = (dk_acc[1] * scale).astype(jnp.bfloat16)
    dfirst_ref[0, 1] = dv_acc[1].astype(jnp.bfloat16)
    dprev_ref[0, 0] = (dk_acc[2] * scale).astype(jnp.bfloat16)
    dprev_ref[0, 1] = dv_acc[2].astype(jnp.bfloat16)


def piece_spec(given):
    stack, at = given
    return pl.BlockSpec((1, *stack.shape[1:]), lambda h, f: (at, 0, 0, 0))


def attn_call(flags, q, g, ko, vo, near, far, befores, outs, heads, scale):
    rows, width = q.shape
    count = len(heads)
    stride = heads[1] - heads[0] if count > 1 else 0
    base = heads[0]
    sub = 112 if rows % 112 == 0 else 16
    column = pl.BlockSpec((rows, D_HEAD), lambda h, f: (0, base + stride * h))
    pair = pl.BlockSpec((1, 2, rows, D_HEAD), lambda h, f: (h, 0, 0, 0))
    given = [near, far, *befores]
    whole = jax.ShapeDtypeStruct((rows, width), jnp.bfloat16)
    piece = jax.ShapeDtypeStruct((count, 2, rows, D_HEAD), jnp.bfloat16)
    passed = [] if outs is None else list(outs)
    aliases = {11 + i: i for i in range(len(passed))}
    flops = 2 * 5 * 3 * rows * rows * D_HEAD * count
    return pl.pallas_call(
        functools.partial(attn_kernel, scale, rows, sub),
        grid_spec=pltpu.PrefetchScalarGridSpec(
            num_scalar_prefetch=1,
            grid=(count,),
            in_specs=[column] * 4 + [piece_spec(x) for x in given]
            + [pl.BlockSpec(memory_space=pl.ANY)] * len(passed),
            out_specs=[column, column, column, pair, pair],
            scratch_shapes=[
                pltpu.VMEM((2, rows, D_HEAD), jnp.bfloat16),
                pltpu.VMEM((2, rows, D_HEAD), jnp.bfloat16),
                pltpu.VMEM((3, D_HEAD, rows), jnp.bfloat16),
                pltpu.VMEM((2, 3, rows, Q_TILE), jnp.float32),
                pltpu.VMEM((2, 3, rows, Q_TILE), jnp.float32),
                pltpu.VMEM((2, 2, 3, rows, Q_TILE), jnp.bfloat16),
                pltpu.VMEM((3, rows, D_HEAD), jnp.float32),
                pltpu.VMEM((3, rows, D_HEAD), jnp.float32),
            ],
        ),
        out_shape=[whole, whole, whole, piece, piece],
        input_output_aliases=aliases,
        compiler_params=pltpu.CompilerParams(
            dimension_semantics=("arbitrary",), vmem_limit_bytes=44 * 1024 * 1024
        ),
        cost_estimate=pl.CostEstimate(
            flops=2 * flops,
            bytes_accessed=15 * rows * D_HEAD * 2 * count,
            transcendentals=3 * rows * rows * count,
        ),
    )(flags, q, g, ko, vo, *[x[0] for x in given], *passed)


def join_kernel(flags_ref, dk_ref, dv_ref, *rest):
    backs, total_ref, dk_out, dv_out = rest[:3], rest[3], rest[4], rest[5]
    owner, side, head = flags_ref[2] > 0, flags_ref[3], pl.program_id(0)
    for i, (src, dst) in enumerate(((dk_ref, dk_out), (dv_ref, dv_out))):
        back = jnp.where(side == 0, backs[1][0, i], backs[2][0, i])
        back = jnp.where(head == 0, backs[0][0, i], back).astype(jnp.float32)
        total = jnp.where(owner & (head == side), total_ref[0, i].astype(jnp.float32), 0.0)
        dst[...] = (src[...].astype(jnp.float32) + back + total).astype(jnp.bfloat16)


def join_call(flags, dk, dv, backs, total, heads):
    rows = dk.shape[0]
    count = len(heads)
    stride = heads[1] - heads[0] if count > 1 else 0
    base = heads[0]
    column = pl.BlockSpec((rows, D_HEAD), lambda h, f: (0, base + stride * h))
    given = [*backs, total]
    whole = jax.ShapeDtypeStruct(dk.shape, jnp.bfloat16)
    return pl.pallas_call(
        join_kernel,
        grid_spec=pltpu.PrefetchScalarGridSpec(
            num_scalar_prefetch=1,
            grid=(count,),
            in_specs=[column, column] + [piece_spec(x) for x in given],
            out_specs=[column, column],
        ),
        out_shape=[whole, whole],
        input_output_aliases={1: 0, 2: 1},
        cost_estimate=pl.CostEstimate(
            flops=4 * rows * D_HEAD * count,
            bytes_accessed=8 * rows * D_HEAD * 2 * count,
            transcendentals=0,
        ),
    )(flags, dk, dv, *[x[0] for x in given])


def pick(index, candidates):
    keys = sorted(candidates)
    out = candidates[keys[0]]
    for k in keys[1:]:
        out = jnp.where(index == k, candidates[k], out)
    return out


def after(value, *others):
    return lax.optimization_barrier((value, *others))[0]


def local(query_in, key_in, value_in, layer_grad, out_weight, group_mask, first_group):
    rows, width = query_in.shape
    heads = width // D_HEAD
    scale = D_HEAD ** (-0.5)
    n = lax.axis_size("tm")
    me = lax.axis_index("tm")
    first = first_group[0]
    owner = first == me
    prev_index = jnp.maximum(me - 1, 0)
    prev_used = (me > 0) & (group_mask[me, prev_index] == 1) & (first != me - 1)
    lines = n // 2
    line, side = me // 2, me % 2
    low_side = side == 0
    hops = (line - first // 2) % lines
    beside = first == (me ^ 1)
    flags = jnp.stack(
        [(~owner).astype(jnp.int32), prev_used.astype(jnp.int32), owner.astype(jnp.int32), side]
    ).astype(jnp.int32)
    count = heads - heads // 2
    chunks = [tuple(range(c, heads, count)) for c in range(count)]
    routes = {
        "swap": [(i, i ^ 1) for i in range(n)],
        "early": [(i, i ^ 1) for i in range(n)],
        "up": [(i, (i + 2) % n) for i in range(n)],
        "down": [((i + 2) % n, i) for i in range(n)],
    }
    lead = lines + 1
    steps = count + lines - 2
    f32, bf16 = jnp.float32, jnp.bfloat16

    def unit(h):
        cols = slice(h * D_HEAD, (h + 1) * D_HEAD)
        return jnp.stack([key_in[:, cols], value_in[:, cols]])

    gathered = lax.all_gather(layer_grad, "head", axis=1, tiled=True)

    sent, came, place = {}, {}, {}

    def out(kind, name, k):
        return sent[kind, k], place[name, k]

    def into(kind, name, k):
        return came[kind, k], place[name, k]

    def read(piece):
        return piece[0][piece[1]]

    def has(c):
        return 0 <= c < count

    own = [(unit(pair[0]), unit(pair[-1])) for pair in chunks]
    firsts, prevs, sums, totals = {}, {}, {}, {}
    outs, attn_grad, done = None, None, []

    def swap_parts(k):
        parts = {}
        c, e = k - lead - 1, k - lead - lines - 1
        extra = 0.0
        if has(e):
            total = sums[e].astype(f32) + read(into("down", "sum", k - 1)).astype(f32)
            totals[e] = total.astype(bf16)
            extra = jnp.where(beside, total, 0.0)
        low_b = own[k][1] if has(k) and k < lines else prevs[c][-1] if has(c) else None
        high_b = None
        if has(k - lines):
            high_b = read(into("up", "next", k - 1))
        elif has(e):
            high_b = (prevs[e][-1].astype(f32) + extra).astype(bf16)
        if has(k) and k < lines:
            parts["a"] = own[k][0]
        if low_b is not None and high_b is not None:
            parts["b"] = jnp.where(low_side, low_b, high_b)
        elif low_b is not None or high_b is not None:
            parts["b"] = high_b if low_b is None else low_b
        if has(e):
            relay = (read(into("down", "back", lead + 2 + e)).astype(f32) + extra).astype(bf16)
            parts["back_a"] = jnp.where(low_side, relay, prevs[e][0])
        c = k - lines
        if has(c):
            choice = {0: read(out("up", "stream", c + 1))}
            choice.update({d: read(into("up", "stream", c + d)) for d in range(1, lines)})
            parts["first"] = pick(hops, choice)
        c = k - lead - 1
        if has(c):
            parts["share"] = jnp.where(low_side, firsts[c][-1], firsts[c][0])
        return parts

    def early_parts(k):
        return {"a": own[k][0], "own_b": own[k][1]} if has(k) and k >= lines else {}

    def other_a(c):
        return into("swap" if c < lines else "early", "a", c)

    def other_b(c):
        return into("swap", "b", c) if c < lines else into("early", "own_b", c)

    def up_parts(k):
        parts = {}
        c = k - 1
        if has(c):
            fresh = jnp.where(
                low_side,
                jnp.where(owner, own[c][0], read(other_a(c))),
                jnp.where(owner, own[c][1], read(other_b(c))),
            )
            parts["stream"] = fresh
        if 0 < c < steps:
            passed = read(into("up", "stream", k - 1))
            parts["stream"] = jnp.where(hops == 0, fresh, passed) if has(c) else passed
        c = k - lines + 1
        if has(c):
            parts["next"] = jnp.where(low_side, read(other_a(c)), own[c][1])
        return parts

    def down_parts(k):
        parts = {}
        s = k - lead - 2
        if has(s):
            mine = jnp.where(low_side, firsts[s][0], firsts[s][-1]).astype(f32)
            share = read(into("swap", "share", k - 1)).astype(f32)
            sums[s] = after((mine + share).astype(bf16))
            parts["back"] = jnp.where(
                low_side, prevs[s][0], read(into("swap", "b", k - 1))
            )
        if 0 <= s < steps:
            low = max(0, s - lines + 1)
            at = s - lines + 1 + hops
            total = pick(at, {c: sums[c] for c in range(low, min(s, count - 1) + 1)})
            if s > 0:
                carried = read(into("down", "sum", k - 1)).astype(f32)
                carried = jnp.where(hops == lines - 1, 0.0, carried)
                total = (total.astype(f32) + carried).astype(bf16)
            parts["sum"] = total
        return parts

    for k in range(lead + count + lines + 2):
        stacks = {}
        for kind, parts in (
            ("early", early_parts(k)), ("swap", swap_parts(k)), ("up", up_parts(k)), ("down", down_parts(k))
        ):
            for i, name in enumerate(parts):
                place[name, k] = i
            if parts:
                stacks[kind] = jnp.stack(list(parts.values()))
        if "early" in stacks:
            came["early", k] = lax.ppermute(stacks.pop("early"), "tm", routes["early"])
        kinds = list(stacks)
        if lines <= k <= lead + count and kinds:
            held = lax.optimization_barrier((*[stacks[x] for x in kinds], *done))
            stacks = dict(zip(kinds, held))
        for kind, stack in stacks.items():
            sent[kind, k] = stack
            came[kind, k] = lax.ppermute(stack, "tm", routes[kind])
        if k > lead + count and "down" in kinds and "swap" in kinds:
            came["down", k] = after(came["down", k], sent["swap", k])
        done = []
        ready = [sent[x, k] for x in kinds]
        if k == lines:
            attn_grad = lax.dot_general(
                after(gathered, *ready), out_weight, (((1,), (1,)), ((), ())),
                preferred_element_type=f32,
            ).astype(bf16)
            for kind in kinds:
                came[kind, k] = after(came[kind, k], attn_grad)
        c = k - lead
        if has(c):
            befores = (
                into("up", "next", c + lines - 1), other_a(c),
                into("swap", "b", c + lines), other_b(c),
            )
            results = attn_call(
                after(flags, *ready), query_in, attn_grad, key_in, value_in,
                out("swap", "first", c + lines), into("swap", "first", c + lines),
                befores, outs, chunks[c], scale,
            )
            outs, firsts[c], prevs[c] = results[:3], results[3], results[4]
            done.append(results[3])
        c = k - lead - lines - 2
        if has(c):
            returned = (
                into("swap", "back_a", k - 1), into("swap", "b", k - 1),
                into("down", "back", lead + 2 + c),
            )
            dq, dk, dv = outs
            dk, dv = join_call(
                flags, dk, dv, returned,
                (totals[c][None], 0), chunks[c],
            )
            outs = (dq, dk, dv)
    return tuple(outs)


def solution(mesh):
    placed = (
        P("tm", "head"),
        P("tm", "head"),
        P("tm", "head"),
        P("tm", "head"),
        P("head", None),
        P(),
        P(),
    )
    return jax.shard_map(
        local,
        mesh=mesh,
        in_specs=placed,
        out_specs=(P("tm", "head"), P("tm", "head"), P("tm", "head")),
        check_vma=False,
    )
```
